32 devices in a mesh: row: 4 (over z), col: 4 (over x, core), depth: 2 (over y).
Axes of the slice: x: 2, y: 2, z: 4, core: 2. Of those that a mesh axis runs over, the one named last changes fastest.
Arguments:
- tokens: bfloat16 [128, 12288], P('depth', 'row'), may hold values from -6 to 6
- w_in: bfloat16 [12288, 24576], P('row', ('col', 'depth')), may hold values from -0.0546875 to 0.0546875
- w_out: bfloat16 [24576, 12288], P(('col', 'depth'), 'row'), may hold values from -0.0390625 to 0.0390625
- cotangent: bfloat16 [128, 12288], P('depth', 'row'), may hold values from -6 to 6
Outputs:
- output: bfloat16 [128, 12288], P(('col', 'depth'), 'row')
- grad_input: bfloat16 [128, 12288], P(('col', 'depth'), 'row')
- grad_w_in: bfloat16 [12288, 24576], P('row', ('col', 'depth'))
- grad_w_out: bfloat16 [24576, 12288], P(('col', 'depth'), 'row')
The draws below stay inside these ranges and needn't reach their ends.
All inputs are finite; a program needn't handle non-finite values.
Results may differ from the reference program's by a relative error of at most 0.019.
Values may be sent and summed in bfloat16 or wider, within the bound.
A program may use at most 192 MiB of HBM per device.

```python
import math
import jax
import jax.numpy as jnp
from jax import lax

D = 12288
FF = 24576
TOKENS = 128
N_ROW = 4
N_COL = 4
N_DEPTH = 2


def shard_levels(own_key, extent, shards, least, top_value):
    gain = 1.0
    for axis_at, shards_of in shards:
        heights = jax.random.uniform(jax.random.fold_in(jax.random.fold_in(own_key, 6), axis_at), (shards_of,), jnp.float32, least / len(shards), top_value / len(shards))
        gain = gain * jnp.repeat(jnp.exp(heights), extent[axis_at] // shards_of).reshape((-1,) + (1,) * (len(extent) - 1 - axis_at))
    return gain


def noise(own_key, dims, scale, most, pieces=(), held_as=jnp.bfloat16):
    factor_of = shard_levels(own_key, dims, pieces, -0.22, 0.18) if pieces else 1.0
    array = jax.random.normal(own_key, dims, jnp.float32) * scale * factor_of
    return jnp.minimum(jnp.maximum(array, -most), most).astype(held_as)


def setup_inputs(seed: int = 0) -> dict:
    streams_of = jax.random.split(jax.random.key(seed), 5)
    tokens = noise(streams_of[0], (TOKENS, D), 1.0, 6.0, ((0, 2), (1, 4)))
    w_in = noise(streams_of[1], (D, FF), D ** -0.5, 0.0546875, ((0, 4), (1, 8)))
    w_out = noise(streams_of[2], (FF, D), FF ** -0.5, 0.0390625, ((0, 8), (1, 4)))
    cotangent = noise(streams_of[3], (TOKENS, D), 1.0, 6.0, ((0, 2), (1, 4)))
    return dict(tokens=tokens, w_in=w_in, w_out=w_out, cotangent=cotangent)


gelu_coef = math.sqrt(2.0 / math.pi)

def gelu_parts(preact):
    inner = gelu_coef * (preact + 0.044715 * preact * preact * preact)
    tanh_val = jnp.tanh(inner)
    gelu_value = 0.5 * preact * (1.0 + tanh_val)
    gelu_slope = 0.5 * (1.0 + tanh_val) + 0.5 * preact * (1.0 - tanh_val * tanh_val) * gelu_coef * (1.0 + 3.0 * 0.044715 * preact * preact)
    return (gelu_value, gelu_slope)

def contract_rows(left, right):
    return lax.dot_general(left, right, (((0,), (0,)), ((), ())), preferred_element_type=jnp.float32)

def contract_cols(left, right):
    return lax.dot_general(left, right, (((1,), (1,)), ((), ())), preferred_element_type=jnp.float32)

def rounded(value):
    return lax.optimization_barrier(value.astype(jnp.bfloat16)).astype(jnp.float32)

def reference(tokens, w_in, w_out, cotangent):
    feat_block = D // N_ROW
    hid_count = N_COL * N_DEPTH
    hid_block = FF // hid_count
    grad_scale = TOKENS ** (-0.5)
    preact = jnp.zeros((TOKENS, FF), jnp.float32)
    act_grad = jnp.zeros((TOKENS, FF), jnp.float32)
    for index in range(N_ROW):
        low = index * feat_block
        high = low + feat_block
        preact = preact + rounded(jnp.dot(tokens[:, low:high], w_in[low:high], preferred_element_type=jnp.float32))
        act_grad = act_grad + rounded(contract_cols(cotangent[:, low:high], w_out[:, low:high]))
    gelu_value, gelu_slope = gelu_parts(preact)
    activation = gelu_value.astype(jnp.bfloat16)
    hidden_grad = (act_grad * gelu_slope).astype(jnp.bfloat16)
    output = jnp.zeros((TOKENS, D), jnp.float32)
    grad_input = jnp.zeros((TOKENS, D), jnp.float32)
    for index in range(hid_count):
        low = index * hid_block
        high = low + hid_block
        output = output + rounded(jnp.dot(activation[:, low:high], w_out[low:high], preferred_element_type=jnp.float32))
        grad_input = grad_input + rounded(contract_cols(hidden_grad[:, low:high], w_in[:, low:high]))
    grad_w_in = contract_rows(tokens, hidden_grad)
    grad_w_out = contract_rows(activation, cotangent)
    return (output.astype(jnp.bfloat16), grad_input.astype(jnp.bfloat16), (grad_w_in * grad_scale).astype(jnp.bfloat16), (grad_w_out * grad_scale).astype(jnp.bfloat16))
```

```python
import functools
import math

import jax
import jax.numpy as jnp
from jax import lax
from jax.experimental import pallas as pl
from jax.experimental.pallas import tpu as pltpu
from jax.sharding import PartitionSpec as P

MESH = pl.DeviceIdType.MESH
CHUNK = 256
TILE = 768
HOP = 2

gelu_coef = math.sqrt(2.0 / math.pi)


def gelu_parts(preact):
    inner = gelu_coef * (preact + 0.044715 * preact * preact * preact)
    tanh_val = jnp.tanh(inner)
    gelu_value = 0.5 * preact * (1.0 + tanh_val)
    gelu_slope = 0.5 * (1.0 + tanh_val) + 0.5 * preact * (1.0 - tanh_val * tanh_val) * gelu_coef * (
        1.0 + 3.0 * 0.044715 * preact * preact
    )
    return (gelu_value, gelu_slope)


def contract_rows(left, right):
    return lax.dot_general(
        left, right, (((0,), (0,)), ((), ())), preferred_element_type=jnp.float32
    )


def contract_cols(left, right):
    return lax.dot_general(
        left, right, (((1,), (1,)), ((), ())), preferred_element_type=jnp.float32
    )


def kernel(
    n_row,
    n_col,
    n_depth,
    tok_ref,
    w_in_ref,
    w_out_ref,
    cot_ref,
    out_ref,
    gin_ref,
    tok_out,
    cot_out,
    act_out,
    hid_out,
    w_in_v,
    w_out_v,
    tok_all,
    cot_all,
    own,
    from_left,
    from_right,
    to_right,
    to_left,
    total,
    slope,
    act_all,
    hid_all,
    acc_out,
    acc_gin,
    pair_send,
    pair_recv,
    part_send,
    part_recv,
    w_in_sem,
    w_out_sem,
    keep_sem,
    left_sems,
    right_sems,
    depth_sems,
    swap_sems,
    pair_sems,
    part_sems,
):
    row = lax.axis_index("row")
    col = lax.axis_index("col")
    depth = lax.axis_index("depth")
    side = lax.rem(col, 2)
    half_col = col // 2
    mate = col + 1 - 2 * side
    slice_rows = tok_ref.shape[0]
    half_rows = slice_rows // 2
    ff = w_in_ref.shape[1]
    d_model = w_in_ref.shape[0]
    steps = ff // CHUNK
    msgs = 2 * steps
    group = (n_col // 2) * n_depth
    me = half_col * n_depth + depth
    block_rows = acc_out.shape[0] // n_col
    piece_rows = block_rows // n_depth
    last_row = n_row - 1

    def cols(j):
        return pl.ds(pl.multiple_of(j * CHUNK, CHUNK), CHUNK)

    def w_in_copy(j):
        return pltpu.make_async_copy(w_in_ref.at[:, cols(j)], w_in_v.at[j], w_in_sem.at[j])

    def w_out_copy(j):
        return pltpu.make_async_copy(w_out_ref.at[cols(j), :], w_out_v.at[j], w_out_sem.at[j])

    @pl.loop(0, steps)
    def _(j):
        w_in_copy(j).start()

    def place(index):
        return {"col": 2 * (index // n_depth) + side, "depth": lax.rem(index, n_depth)}

    barrier = pltpu.get_barrier_semaphore()

    @pl.when(row > 0)
    def _():
        pl.semaphore_signal(barrier, inc=1, device_id={"row": row - 1}, device_id_type=MESH)

    @pl.when(row < last_row)
    def _():
        pl.semaphore_signal(barrier, inc=1, device_id={"row": row + 1}, device_id_type=MESH)

    pl.semaphore_signal(barrier, inc=1, device_id={"col": mate}, device_id_type=MESH)
    for k in range(1, group):
        pl.semaphore_signal(
            barrier, inc=1, device_id=place(lax.rem(me + k, group)), device_id_type=MESH
        )
    own_rows = pl.ds(pl.multiple_of(depth * slice_rows, slice_rows), slice_rows)
    tok_all[own_rows, :] = tok_ref[...]
    cot_all[own_rows, :] = cot_ref[...]
    acc_out[...] = jnp.zeros_like(acc_out)
    acc_gin[...] = jnp.zeros_like(acc_gin)

    edges = jnp.where(row > 0, 1, 0) + jnp.where(row < last_row, 1, 0)
    pl.semaphore_wait(barrier, group + edges)

    def depth_copy(a, k):
        src, dst = ((tok_ref, tok_all), (cot_ref, cot_all))[a]
        here = pl.multiple_of(side * half_rows, half_rows)
        there = pl.multiple_of(depth * slice_rows + side * half_rows, half_rows)
        return pltpu.make_async_remote_copy(
            src_ref=src.at[pl.ds(here, half_rows), :],
            dst_ref=dst.at[pl.ds(there, half_rows), :],
            send_sem=depth_sems.at[0, a, k - 1],
            recv_sem=depth_sems.at[1, a, k - 1],
            device_id={"depth": lax.rem(depth + k, n_depth)},
            device_id_type=MESH,
        )

    def swap_copy(a, k):
        dst = (tok_all, cot_all)[a]
        origin = lax.rem(depth + n_depth - k, n_depth)
        rows = pl.ds(pl.multiple_of(origin * slice_rows + side * half_rows, half_rows), half_rows)
        return pltpu.make_async_remote_copy(
            src_ref=dst.at[rows, :],
            dst_ref=dst.at[rows, :],
            send_sem=swap_sems.at[0, a, k - 1],
            recv_sem=swap_sems.at[1, a, k - 1],
            device_id={"col": mate},
            device_id_type=MESH,
        )

    for a in range(2):
        for k in range(1, n_depth):
            depth_copy(a, k).start()

    def pass_on(a):
        for k in range(1, n_depth):
            depth_copy(a, k).wait_recv()
            swap_copy(a, k).start()

    def arrived(a):
        for k in range(1, n_depth):
            swap_copy(a, k).wait_recv()

    def right_copy(m):
        return pltpu.make_async_remote_copy(
            src_ref=to_right.at[m],
            dst_ref=from_left.at[m],
            send_sem=left_sems.at[0, m],
            recv_sem=left_sems.at[1, m],
            device_id={"row": lax.rem(row + 1, n_row)},
            device_id_type=MESH,
        )

    def left_copy(m):
        return pltpu.make_async_remote_copy(
            src_ref=to_left.at[m],
            dst_ref=from_right.at[m],
            send_sem=right_sems.at[0, m],
            recv_sem=right_sems.at[1, m],
            device_id={"row": lax.rem(row + n_row - 1, n_row)},
            device_id_type=MESH,
        )

    def pair_copy(a, i):
        return pltpu.make_async_remote_copy(
            src_ref=pair_send.at[a, i],
            dst_ref=pair_recv.at[a, i],
            send_sem=pair_sems.at[0, a, i],
            recv_sem=pair_sems.at[1, a, i],
            device_id={"col": mate},
            device_id_type=MESH,
        )

    def part_copy(a, k):
        return pltpu.make_async_remote_copy(
            src_ref=part_send.at[a, lax.rem(me + k, group)],
            dst_ref=part_recv.at[a, k - 1],
            send_sem=part_sems.at[0, a, k - 1],
            recv_sem=part_sems.at[1, a, k - 1],
            device_id=place(lax.rem(me + k, group)),
            device_id_type=MESH,
        )

    def send_pair(a, acc):
        for i in range(n_col // 2):
            rows = pl.ds(pl.multiple_of((2 * i + 1 - side) * block_rows, block_rows), block_rows)
            pair_send[a, i] = acc[rows, :].astype(jnp.bfloat16)
            pair_copy(a, i).start()

    def send_parts(a, acc):
        for i in range(n_col // 2):
            pair_copy(a, i).wait_recv()
            for p in range(n_depth):
                rows = pl.ds(
                    pl.multiple_of((2 * i + side) * block_rows + p * piece_rows, piece_rows),
                    piece_rows,
                )
                part_send[a, i * n_depth + p] = (
                    acc[rows, :]
                    + pair_recv[a, i, p * piece_rows : (p + 1) * piece_rows, :].astype(jnp.float32)
                ).astype(jnp.bfloat16)
        for k in range(1, group):
            part_copy(a, k).start()

    def finish(a, ref):
        result = part_send[a, me].astype(jnp.float32)
        for k in range(1, group):
            part_copy(a, k).wait_recv()
            result = result + part_recv[a, k - 1].astype(jnp.float32)
        ref[...] = result.astype(ref.dtype)

    outs = ((tok_all, tok_out), (cot_all, cot_out), (act_all, act_out), (hid_all, hid_out))

    def keep(a):
        return pltpu.make_async_copy(outs[a][0], outs[a][1], keep_sem.at[a])

    pass_on(0)
    arrived(0)
    keep(0).start()

    far = jnp.maximum(row, last_row - row)
    wait_lag = min(steps, HOP * (n_row // 2))

    @pl.loop(0, msgs + HOP * last_row)
    def _(t):
        @pl.when(t < steps)
        def _():
            w_out_copy(t).start()
            w_in_copy(t).wait()
            own[t] = jnp.dot(
                tok_all[...], w_in_v[t], preferred_element_type=jnp.float32
            ).astype(jnp.bfloat16)

        ready = t - wait_lag

        @pl.when(jnp.logical_and(ready >= 0, ready < steps))
        def _():
            w_out_copy(ready).wait()

        @pl.when(t == min(4, steps - 1))
        def _():
            pass_on(1)

        @pl.when(t == steps)
        def _():
            arrived(1)
            keep(1).start()

        @pl.when(jnp.logical_and(t >= steps, t < msgs))
        def _():
            own[t] = contract_cols(cot_all[...], w_out_v[t - steps]).astype(jnp.bfloat16)

        m1 = t - HOP * row

        @pl.when(jnp.logical_and(m1 >= 0, m1 < msgs))
        def _():
            @pl.when(row == 0)
            def _():
                to_right[m1] = own[m1]

            @pl.when(row > 0)
            def _():
                right_copy(m1).wait_recv()

                @pl.when(row < last_row)
                def _():
                    to_right[m1] = (
                        own[m1].astype(jnp.float32) + from_left[m1].astype(jnp.float32)
                    ).astype(jnp.bfloat16)

            @pl.when(row < last_row)
            def _():
                right_copy(m1).start()

        m2 = t - HOP * (last_row - row)

        @pl.when(jnp.logical_and(m2 >= 0, m2 < msgs))
        def _():
            @pl.when(row == last_row)
            def _():
                to_left[m2] = own[m2]

            @pl.when(row < last_row)
            def _():
                left_copy(m2).wait_recv()

                @pl.when(row > 0)
                def _():
                    to_left[m2] = (
                        own[m2].astype(jnp.float32) + from_right[m2].astype(jnp.float32)
                    ).astype(jnp.bfloat16)

            @pl.when(row > 0)
            def _():
                left_copy(m2).start()

        m = t - HOP * far

        @pl.when(jnp.logical_and(m >= 0, m < msgs))
        def _():
            total[...] = own[m].astype(jnp.float32)

            @pl.when(row > 0)
            def _():
                total[...] += from_left[m].astype(jnp.float32)

            @pl.when(row < last_row)
            def _():
                total[...] += from_right[m].astype(jnp.float32)

        @pl.when(jnp.logical_and(m >= 0, m < steps))
        def _():
            value, slope_value = gelu_parts(total[...])
            slope[m] = slope_value
            block = value.astype(jnp.bfloat16)
            act_all[:, cols(m)] = block
            for n in range(0, d_model, TILE):
                acc_out[:, n : n + TILE] += jnp.dot(
                    block, w_out_v[m, :, n : n + TILE], preferred_element_type=jnp.float32
                )

        mo = m - steps

        @pl.when(jnp.logical_and(mo >= 0, mo < steps))
        def _():
            grad = (total[...] * slope[mo]).astype(jnp.bfloat16)
            hid_all[:, cols(mo)] = grad
            for n in range(0, d_model, TILE):
                acc_gin[:, n : n + TILE] += contract_cols(grad, w_in_v[mo, n : n + TILE, :])

        @pl.when(m == steps)
        def _():
            keep(2).start()
            send_pair(0, acc_out)

        @pl.when(m == steps + min(2, steps - 1))
        def _():
            send_parts(0, acc_out)

    keep(3).start()
    send_pair(1, acc_gin)
    send_parts(1, acc_gin)
    finish(0, out_ref)
    finish(1, gin_ref)

    for a in range(4):
        keep(a).wait()
    for a in range(2):
        for k in range(1, n_depth):
            depth_copy(a, k).wait_send()
            swap_copy(a, k).wait_send()
        for i in range(n_col // 2):
            pair_copy(a, i).wait_send()
        for k in range(1, group):
            part_copy(a, k).wait_send()

    @pl.loop(0, msgs)
    def _(m):
        @pl.when(row < last_row)
        def _():
            right_copy(m).wait_send()

        @pl.when(row > 0)
        def _():
            left_copy(m).wait_send()


def exchange(sizes, tokens, w_in, w_out, cotangent):
    n_row, n_col, n_depth = sizes
    slice_rows, d_model = tokens.shape
    rows = slice_rows * n_depth
    ff = w_in.shape[1]
    steps = ff // CHUNK
    msgs = 2 * steps
    group = (n_col // 2) * n_depth
    block_rows = rows // n_col
    piece_rows = block_rows // n_depth
    bf16, f32 = jnp.bfloat16, jnp.float32
    vmem = pl.BlockSpec(memory_space=pltpu.VMEM)
    hbm = pl.BlockSpec(memory_space=pl.ANY)
    dma = pltpu.SemaphoreType.DMA
    return pl.pallas_call(
        functools.partial(kernel, n_row, n_col, n_depth),
        out_shape=(
            jax.ShapeDtypeStruct((piece_rows, d_model), bf16),
            jax.ShapeDtypeStruct((piece_rows, d_model), bf16),
            jax.ShapeDtypeStruct((rows, d_model), bf16),
            jax.ShapeDtypeStruct((rows, d_model), bf16),
            jax.ShapeDtypeStruct((rows, ff), bf16),
            jax.ShapeDtypeStruct((rows, ff), bf16),
        ),
        in_specs=[vmem, hbm, hbm, vmem],
        out_specs=(vmem, vmem, hbm, hbm, hbm, hbm),
        scratch_shapes=[
            pltpu.VMEM((steps, d_model, CHUNK), bf16),
            pltpu.VMEM((steps, CHUNK, d_model), bf16),
            pltpu.VMEM((rows, d_model), bf16),
            pltpu.VMEM((rows, d_model), bf16),
            pltpu.VMEM((msgs, rows, CHUNK), bf16),
            pltpu.VMEM((msgs, rows, CHUNK), bf16),
            pltpu.VMEM((msgs, rows, CHUNK), bf16),
            pltpu.VMEM((msgs, rows, CHUNK), bf16),
            pltpu.VMEM((msgs, rows, CHUNK), bf16),
            pltpu.VMEM((rows, CHUNK), f32),
            pltpu.VMEM((steps, rows, CHUNK), f32),
            pltpu.VMEM((rows, ff), bf16),
            pltpu.VMEM((rows, ff), bf16),
            pltpu.VMEM((rows, d_model), f32),
            pltpu.VMEM((rows, d_model), f32),
            pltpu.VMEM((2, n_col // 2, block_rows, d_model), bf16),
            pltpu.VMEM((2, n_col // 2, block_rows, d_model), bf16),
            pltpu.VMEM((2, group, piece_rows, d_model), bf16),
            pltpu.VMEM((2, group - 1, piece_rows, d_model), bf16),
            dma((steps,)),
            dma((steps,)),
            dma((4,)),
            dma((2, msgs)),
            dma((2, msgs)),
            dma((2, 2, n_depth - 1)),
            dma((2, 2, n_depth - 1)),
            dma((2, 2, n_col // 2)),
            dma((2, 2, group - 1)),
        ],
        compiler_params=pltpu.CompilerParams(
            collective_id=0, has_side_effects=True, vmem_limit_bytes=62 * 2**20
        ),
        cost_estimate=pl.CostEstimate(
            flops=8 * rows * d_model * ff, bytes_accessed=4 * d_model * ff, transcendentals=rows * ff
        ),
        name="exchange",
    )(tokens, w_in, w_out, cotangent)


def body(sizes, tokens, w_in, w_out, cotangent):
    output, grad_input, all_tokens, all_grads, act, hidden = exchange(
        sizes, tokens, w_in, w_out, cotangent
    )
    grad_scale = all_tokens.shape[0] ** (-0.5)
    grad_w_out = (contract_rows(act, all_grads) * grad_scale).astype(jnp.bfloat16)
    grad_w_in = (contract_rows(all_tokens, hidden) * grad_scale).astype(jnp.bfloat16)
    return (output, grad_input, grad_w_in, grad_w_out)


def solution(mesh):
    sizes = (mesh.shape["row"], mesh.shape["col"], mesh.shape["depth"])
    in_specs = (
        P("depth", "row"),
        P("row", ("col", "depth")),
        P(("col", "depth"), "row"),
        P("depth", "row"),
    )
    out_specs = (
        P(("col", "depth"), "row"),
        P(("col", "depth"), "row"),
        P("row", ("col", "depth")),
        P(("col", "depth"), "row"),
    )
    return jax.shard_map(
        functools.partial(body, sizes),
        mesh=mesh,
        in_specs=in_specs,
        out_specs=out_specs,
        check_vma=False,
    )
```

```python
import functools
import math

import jax
import jax.numpy as jnp
from jax import lax
from jax.experimental import pallas as pl
from jax.experimental.pallas import tpu as pltpu
from jax.sharding import PartitionSpec as P

MESH = pl.DeviceIdType.MESH
CHUNK = 256
TILE = 768
HOP = 3
GRAD_ROWS = 512

gelu_coef = math.sqrt(2.0 / math.pi)


def gelu_parts(preact):
    inner = gelu_coef * (preact + 0.044715 * preact * preact * preact)
    tanh_val = jnp.tanh(inner)
    gelu_value = 0.5 * preact * (1.0 + tanh_val)
    gelu_slope = 0.5 * (1.0 + tanh_val) + 0.5 * preact * (1.0 - tanh_val * tanh_val) * gelu_coef * (
        1.0 + 3.0 * 0.044715 * preact * preact
    )
    return (gelu_value, gelu_slope)


def contract_cols(left, right):
    return lax.dot_general(
        left, right, (((1,), (1,)), ((), ())), preferred_element_type=jnp.float32
    )


def kernel(
    n_row,
    n_col,
    n_depth,
    tok_ref,
    w_in_ref,
    w_out_ref,
    cot_ref,
    out_ref,
    gin_ref,
    tok_out,
    cot_out,
    act_out,
    hid_out,
    w_in_v,
    w_out_v,
    tok_all,
    cot_all,
    own,
    from_left,
    from_right,
    to_right,
    to_left,
    total,
    slope,
    act_all,
    hid_all,
    acc_out,
    acc_gin,
    pair_send,
    pair_recv,
    part_send,
    part_recv,
    w_in_sem,
    w_out_sem,
    keep_sem,
    left_sems,
    right_sems,
    depth_sems,
    swap_sems,
    pair_sems,
    part_sems,
):
    row = lax.axis_index("row")
    col = lax.axis_index("col")
    depth = lax.axis_index("depth")
    side = lax.rem(col, 2)
    half_col = col // 2
    mate = col + 1 - 2 * side
    slice_rows = tok_ref.shape[0]
    half_rows = slice_rows // 2
    ff = w_in_ref.shape[1]
    d_model = w_in_ref.shape[0]
    steps = ff // CHUNK
    msgs = 2 * steps
    group = (n_col // 2) * n_depth
    me = half_col * n_depth + depth
    block_rows = acc_out.shape[0] // n_col
    piece_rows = block_rows // n_depth
    last_row = n_row - 1

    def cols(j):
        return pl.ds(pl.multiple_of(j * CHUNK, CHUNK), CHUNK)

    def w_in_copy(j):
        return pltpu.make_async_copy(w_in_ref.at[:, cols(j)], w_in_v.at[j], w_in_sem.at[j])

    def w_out_copy(j):
        return pltpu.make_async_copy(w_out_ref.at[cols(j), :], w_out_v.at[j], w_out_sem.at[j])

    @pl.loop(0, steps)
    def _(j):
        w_in_copy(j).start()

    def place(index):
        return {"col": 2 * (index // n_depth) + side, "depth": lax.rem(index, n_depth)}

    barrier = pltpu.get_barrier_semaphore()

    @pl.when(row > 0)
    def _():
        pl.semaphore_signal(barrier, inc=1, device_id={"row": row - 1}, device_id_type=MESH)

    @pl.when(row < last_row)
    def _():
        pl.semaphore_signal(barrier, inc=1, device_id={"row": row + 1}, device_id_type=MESH)

    pl.semaphore_signal(barrier, inc=1, device_id={"col": mate}, device_id_type=MESH)
    for k in range(1, group):
        pl.semaphore_signal(
            barrier, inc=1, device_id=place(lax.rem(me + k, group)), device_id_type=MESH
        )
    own_rows = pl.ds(pl.multiple_of(depth * slice_rows, slice_rows), slice_rows)
    tok_all[own_rows, :] = tok_ref[...]
    cot_all[own_rows, :] = cot_ref[...]
    acc_out[...] = jnp.zeros_like(acc_out)
    acc_gin[...] = jnp.zeros_like(acc_gin)

    edges = jnp.where(row > 0, 1, 0) + jnp.where(row < last_row, 1, 0)
    pl.semaphore_wait(barrier, group + edges)

    def depth_copy(a, k):
        src, dst = ((tok_ref, tok_all), (cot_ref, cot_all))[a]
        here = pl.multiple_of(side * half_rows, half_rows)
        there = pl.multiple_of(depth * slice_rows + side * half_rows, half_rows)
        return pltpu.make_async_remote_copy(
            src_ref=src.at[pl.ds(here, half_rows), :],
            dst_ref=dst.at[pl.ds(there, half_rows), :],
            send_sem=depth_sems.at[0, a, k - 1],
            recv_sem=depth_sems.at[1, a, k - 1],
            device_id={"depth": lax.rem(depth + k, n_depth)},
            device_id_type=MESH,
        )

    def swap_copy(a, k):
        dst = (tok_all, cot_all)[a]
        origin = lax.rem(depth + n_depth - k, n_depth)
        rows = pl.ds(pl.multiple_of(origin * slice_rows + side * half_rows, half_rows), half_rows)
        return pltpu.make_async_remote_copy(
            src_ref=dst.at[rows, :],
            dst_ref=dst.at[rows, :],
            send_sem=swap_sems.at[0, a, k - 1],
            recv_sem=swap_sems.at[1, a, k - 1],
            device_id={"col": mate},
            device_id_type=MESH,
        )

    def spread(a):
        for k in range(1, n_depth):
            depth_copy(a, k).start()

    def pass_on(a):
        for k in range(1, n_depth):
            depth_copy(a, k).wait_recv()
            swap_copy(a, k).start()

    def arrived(a):
        for k in range(1, n_depth):
            swap_copy(a, k).wait_recv()

    def right_copy(m):
        return pltpu.make_async_remote_copy(
            src_ref=to_right.at[m],
            dst_ref=from_left.at[m],
            send_sem=left_sems.at[0, m],
            recv_sem=left_sems.at[1, m],
            device_id={"row": lax.rem(row + 1, n_row)},
            device_id_type=MESH,
        )

    def left_copy(m):
        return pltpu.make_async_remote_copy(
            src_ref=to_left.at[m],
            dst_ref=from_right.at[m],
            send_sem=right_sems.at[0, m],
            recv_sem=right_sems.at[1, m],
            device_id={"row": lax.rem(row + n_row - 1, n_row)},
            device_id_type=MESH,
        )

    def pair_copy(a, i):
        return pltpu.make_async_remote_copy(
            src_ref=pair_send.at[a, i],
            dst_ref=pair_recv.at[a, i],
            send_sem=pair_sems.at[0, a, i],
            recv_sem=pair_sems.at[1, a, i],
            device_id={"col": mate},
            device_id_type=MESH,
        )

    def part_copy(a, k):
        return pltpu.make_async_remote_copy(
            src_ref=part_send.at[a, lax.rem(me + k, group)],
            dst_ref=part_recv.at[a, k - 1],
            send_sem=part_sems.at[0, a, k - 1],
            recv_sem=part_sems.at[1, a, k - 1],
            device_id=place(lax.rem(me + k, group)),
            device_id_type=MESH,
        )

    def send_pair(a, acc):
        for i in range(n_col // 2):
            rows = pl.ds(pl.multiple_of((2 * i + 1 - side) * block_rows, block_rows), block_rows)
            pair_send[a, i] = acc[rows, :].astype(jnp.bfloat16)
            pair_copy(a, i).start()

    def send_parts(a, acc):
        for i in range(n_col // 2):
            pair_copy(a, i).wait_recv()
            for p in range(n_depth):
                rows = pl.ds(
                    pl.multiple_of((2 * i + side) * block_rows + p * piece_rows, piece_rows),
                    piece_rows,
                )
                part_send[a, i * n_depth + p] = (
                    acc[rows, :]
                    + pair_recv[a, i, p * piece_rows : (p + 1) * piece_rows, :].astype(jnp.float32)
                ).astype(jnp.bfloat16)
        for k in range(1, group):
            part_copy(a, k).start()

    def finish(a, ref):
        result = part_send[a, me].astype(jnp.float32)
        for k in range(1, group):
            part_copy(a, k).wait_recv()
            result = result + part_recv[a, k - 1].astype(jnp.float32)
        ref[...] = result.astype(ref.dtype)

    outs = ((tok_all, tok_out), (cot_all, cot_out), (act_all, act_out), (hid_all, hid_out))

    def keep(a):
        return pltpu.make_async_copy(outs[a][0], outs[a][1], keep_sem.at[a])

    spread(0)
    pass_on(0)
    spread(1)
    arrived(0)
    keep(0).start()

    far = jnp.maximum(row, last_row - row)
    wait_lag = min(steps, HOP * (n_row // 2))

    @pl.loop(0, msgs + HOP * last_row)
    def _(t):
        @pl.when(t < steps)
        def _():
            w_out_copy(t).start()
            w_in_copy(t).wait()
            own[t] = jnp.dot(
                tok_all[...], w_in_v[t], preferred_element_type=jnp.float32
            ).astype(jnp.bfloat16)

        ready = t - wait_lag

        @pl.when(jnp.logical_and(ready >= 0, ready < steps))
        def _():
            w_out_copy(ready).wait()

        @pl.when(t == min(4, steps - 1))
        def _():
            pass_on(1)

        @pl.when(t == steps)
        def _():
            arrived(1)
            keep(1).start()

        @pl.when(jnp.logical_and(t >= steps, t < msgs))
        def _():
            own[t] = contract_cols(cot_all[...], w_out_v[t - steps]).astype(jnp.bfloat16)

        m1 = t - HOP * row

        @pl.when(jnp.logical_and(m1 >= 0, m1 < msgs))
        def _():
            @pl.when(row == 0)
            def _():
                to_right[m1] = own[m1]

            @pl.when(row > 0)
            def _():
                right_copy(m1).wait_recv()

                @pl.when(row < last_row)
                def _():
                    to_right[m1] = (
                        own[m1].astype(jnp.float32) + from_left[m1].astype(jnp.float32)
                    ).astype(jnp.bfloat16)

            @pl.when(row < last_row)
            def _():
                right_copy(m1).start()

        m2 = t - HOP * (last_row - row)

        @pl.when(jnp.logical_and(m2 >= 0, m2 < msgs))
        def _():
            @pl.when(row == last_row)
            def _():
                to_left[m2] = own[m2]

            @pl.when(row < last_row)
            def _():
                left_copy(m2).wait_recv()

                @pl.when(row > 0)
                def _():
                    to_left[m2] = (
                        own[m2].astype(jnp.float32) + from_right[m2].astype(jnp.float32)
                    ).astype(jnp.bfloat16)

            @pl.when(row > 0)
            def _():
                left_copy(m2).start()

        m = t - HOP * far

        @pl.when(jnp.logical_and(m >= 0, m < msgs))
        def _():
            total[...] = own[m].astype(jnp.float32)

            @pl.when(row > 0)
            def _():
                total[...] += from_left[m].astype(jnp.float32)

            @pl.when(row < last_row)
            def _():
                total[...] += from_right[m].astype(jnp.float32)

        @pl.when(jnp.logical_and(m >= 0, m < steps))
        def _():
            value, slope_value = gelu_parts(total[...])
            slope[m] = slope_value
            block = value.astype(jnp.bfloat16)
            act_all[:, cols(m)] = block
            for n in range(0, d_model, TILE):
                acc_out[:, n : n + TILE] += jnp.dot(
                    block, w_out_v[m, :, n : n + TILE], preferred_element_type=jnp.float32
                )

        mo = m - steps

        @pl.when(jnp.logical_and(mo >= 0, mo < steps))
        def _():
            grad = (total[...] * slope[mo]).astype(jnp.bfloat16)
            hid_all[:, cols(mo)] = grad
            for n in range(0, d_model, TILE):
                acc_gin[:, n : n + TILE] += contract_cols(grad, w_in_v[mo, n : n + TILE, :])

        @pl.when(m == steps)
        def _():
            keep(2).start()
            send_pair(0, acc_out)

        @pl.when(m == steps + min(2, steps - 1))
        def _():
            send_parts(0, acc_out)

    keep(3).start()
    send_pair(1, acc_gin)
    send_parts(1, acc_gin)
    finish(0, out_ref)
    finish(1, gin_ref)

    for a in range(4):
        keep(a).wait()
    for a in range(2):
        for k in range(1, n_depth):
            depth_copy(a, k).wait_send()
            swap_copy(a, k).wait_send()
        for i in range(n_col // 2):
            pair_copy(a, i).wait_send()
        for k in range(1, group):
            part_copy(a, k).wait_send()

    @pl.loop(0, msgs)
    def _(m):
        @pl.when(row < last_row)
        def _():
            right_copy(m).wait_send()

        @pl.when(row > 0)
        def _():
            left_copy(m).wait_send()


def exchange(sizes, tokens, w_in, w_out, cotangent):
    n_row, n_col, n_depth = sizes
    slice_rows, d_model = tokens.shape
    rows = slice_rows * n_depth
    ff = w_in.shape[1]
    steps = ff // CHUNK
    msgs = 2 * steps
    group = (n_col // 2) * n_depth
    block_rows = rows // n_col
    piece_rows = block_rows // n_depth
    bf16, f32 = jnp.bfloat16, jnp.float32
    vmem = pl.BlockSpec(memory_space=pltpu.VMEM)
    hbm = pl.BlockSpec(memory_space=pl.ANY)
    dma = pltpu.SemaphoreType.DMA
    return pl.pallas_call(
        functools.partial(kernel, n_row, n_col, n_depth),
        out_shape=(
            jax.ShapeDtypeStruct((piece_rows, d_model), bf16),
            jax.ShapeDtypeStruct((piece_rows, d_model), bf16),
            jax.ShapeDtypeStruct((rows, d_model), bf16),
            jax.ShapeDtypeStruct((rows, d_model), bf16),
            jax.ShapeDtypeStruct((rows, ff), bf16),
            jax.ShapeDtypeStruct((rows, ff), bf16),
        ),
        in_specs=[vmem, hbm, hbm, vmem],
        out_specs=(vmem, vmem, hbm, hbm, hbm, hbm),
        scratch_shapes=[
            pltpu.VMEM((steps, d_model, CHUNK), bf16),
            pltpu.VMEM((steps, CHUNK, d_model), bf16),
            pltpu.VMEM((rows, d_model), bf16),
            pltpu.VMEM((rows, d_model), bf16),
            pltpu.VMEM((msgs, rows, CHUNK), bf16),
            pltpu.VMEM((msgs, rows, CHUNK), bf16),
            pltpu.VMEM((msgs, rows, CHUNK), bf16),
            pltpu.VMEM((msgs, rows, CHUNK), bf16),
            pltpu.VMEM((msgs, rows, CHUNK), bf16),
            pltpu.VMEM((rows, CHUNK), f32),
            pltpu.VMEM((steps, rows, CHUNK), f32),
            pltpu.VMEM((rows, ff), bf16),
            pltpu.VMEM((rows, ff), bf16),
            pltpu.VMEM((rows, d_model), f32),
            pltpu.VMEM((rows, d_model), f32),
            pltpu.VMEM((2, n_col // 2, block_rows, d_model), bf16),
            pltpu.VMEM((2, n_col // 2, block_rows, d_model), bf16),
            pltpu.VMEM((2, group, piece_rows, d_model), bf16),
            pltpu.VMEM((2, group - 1, piece_rows, d_model), bf16),
            dma((steps,)),
            dma((steps,)),
            dma((4,)),
            dma((2, msgs)),
            dma((2, msgs)),
            dma((2, 2, n_depth - 1)),
            dma((2, 2, n_depth - 1)),
            dma((2, 2, n_col // 2)),
            dma((2, 2, group - 1)),
        ],
        compiler_params=pltpu.CompilerParams(
            collective_id=0, has_side_effects=True, vmem_limit_bytes=62 * 2**20
        ),
        cost_estimate=pl.CostEstimate(
            flops=8 * rows * d_model * ff, bytes_accessed=4 * d_model * ff, transcendentals=rows * ff
        ),
        name="exchange",
    )(tokens, w_in, w_out, cotangent)


def grads_kernel(scale, tok, hid, act, cot, out, gin, g_in, g_out, out_copy, gin_copy):
    @pl.when(pl.program_id(0) == 0)
    def _():
        out_copy[...] = out[...]
        gin_copy[...] = gin[...]

    for left, right, result in ((tok, hid, g_in), (act, cot, g_out)):
        turned = left[...].T
        for n in range(0, right.shape[1], TILE):
            result[:, n : n + TILE] = (
                jnp.dot(turned, right[:, n : n + TILE], preferred_element_type=jnp.float32) * scale
            ).astype(result.dtype)


def weight_grads(tokens, hidden, act, grads, output, grad_input):
    rows, d_model = tokens.shape
    ff = hidden.shape[1]
    bf16 = jnp.bfloat16
    count = max(d_model, ff) // GRAD_ROWS
    small = pl.BlockSpec(output.shape, lambda i: (0, 0))
    return pl.pallas_call(
        functools.partial(grads_kernel, rows ** (-0.5)),
        grid=(count,),
        out_shape=(
            jax.ShapeDtypeStruct((d_model, ff), bf16),
            jax.ShapeDtypeStruct((ff, d_model), bf16),
            jax.ShapeDtypeStruct(output.shape, bf16),
            jax.ShapeDtypeStruct(grad_input.shape, bf16),
        ),
        in_specs=[
            pl.BlockSpec((rows, d_model // count), lambda i: (0, i)),
            pl.BlockSpec((rows, ff), lambda i: (0, 0)),
            pl.BlockSpec((rows, ff // count), lambda i: (0, i)),
            pl.BlockSpec((rows, d_model), lambda i: (0, 0)),
            small,
            small,
        ],
        out_specs=(
            pl.BlockSpec((d_model // count, ff), lambda i: (i, 0)),
            pl.BlockSpec((ff // count, d_model), lambda i: (i, 0)),
            small,
            small,
        ),
        compiler_params=pltpu.CompilerParams(vmem_limit_bytes=62 * 2**20),
        cost_estimate=pl.CostEstimate(
            flops=4 * rows * d_model * ff, bytes_accessed=4 * d_model * ff, transcendentals=0
        ),
        name="weight_grads",
    )(tokens, hidden, act, grads, output, grad_input)


def body(sizes, tokens, w_in, w_out, cotangent):
    output, grad_input, all_tokens, all_grads, act, hidden = exchange(
        sizes, tokens, w_in, w_out, cotangent
    )
    grad_w_in, grad_w_out, output, grad_input = weight_grads(
        all_tokens, hidden, act, all_grads, output, grad_input
    )
    return (output, grad_input, grad_w_in, grad_w_out)


def solution(mesh):
    sizes = (mesh.shape["row"], mesh.shape["col"], mesh.shape["depth"])
    in_specs = (
        P("depth", "row"),
        P("row", ("col", "depth")),
        P(("col", "depth"), "row"),
        P("depth", "row"),
    )
    out_specs = (
        P(("col", "depth"), "row"),
        P(("col", "depth"), "row"),
        P("row", ("col", "depth")),
        P(("col", "depth"), "row"),
    )
    return jax.shard_map(
        functools.partial(body, sizes),
        mesh=mesh,
        in_specs=in_specs,
        out_specs=out_specs,
        check_vma=False,
    )
```

```python
import functools
import math

import jax
import jax.numpy as jnp
from jax import lax
from jax.experimental import pallas as pl
from jax.experimental.pallas import tpu as pltpu
from jax.sharding import PartitionSpec as P

MESH = pl.DeviceIdType.MESH
CHUNK = 256
TILE = 768
HOP = 3
GRAD_ROWS = 512

gelu_coef = math.sqrt(2.0 / math.pi)


def gelu_parts(preact):
    inner = gelu_coef * (preact + 0.044715 * preact * preact * preact)
    tanh_val = jnp.tanh(inner)
    gelu_value = 0.5 * preact * (1.0 + tanh_val)
    gelu_slope = 0.5 * (1.0 + tanh_val) + 0.5 * preact * (1.0 - tanh_val * tanh_val) * gelu_coef * (
        1.0 + 3.0 * 0.044715 * preact * preact
    )
    return (gelu_value, gelu_slope)


def contract_cols(left, right):
    return lax.dot_general(
        left, right, (((1,), (1,)), ((), ())), preferred_element_type=jnp.float32
    )


def kernel(
    n_row,
    n_col,
    n_depth,
    tok_ref,
    w_in_ref,
    w_out_ref,
    cot_ref,
    out_ref,
    gin_ref,
    tok_out,
    cot_out,
    act_out,
    hid_out,
    w_in_v,
    w_out_v,
    tok_all,
    cot_all,
    own,
    from_left,
    from_right,
    to_right,
    to_left,
    total,
    slope,
    act_all,
    hid_all,
    acc_out,
    acc_gin,
    pair_send,
    pair_recv,
    part_send,
    part_recv,
    w_in_sem,
    w_out_sem,
    keep_sem,
    left_sems,
    right_sems,
    depth_sems,
    swap_sems,
    pair_sems,
    part_sems,
):
    row = lax.axis_index("row")
    col = lax.axis_index("col")
    depth = lax.axis_index("depth")
    side = lax.rem(col, 2)
    half_col = col // 2
    mate = col + 1 - 2 * side
    slice_rows = tok_ref.shape[0]
    half_rows = slice_rows // 2
    ff = w_in_ref.shape[1]
    d_model = w_in_ref.shape[0]
    steps = ff // CHUNK
    msgs = 2 * steps
    group = (n_col // 2) * n_depth
    me = half_col * n_depth + depth
    block_rows = acc_out.shape[0] // n_col
    piece_rows = block_rows // n_depth
    last_row = n_row - 1

    def cols(j):
        return pl.ds(pl.multiple_of(j * CHUNK, CHUNK), CHUNK)

    def w_in_copy(j):
        return pltpu.make_async_copy(w_in_ref.at[:, cols(j)], w_in_v.at[j], w_in_sem.at[j])

    def w_out_copy(j):
        return pltpu.make_async_copy(w_out_ref.at[cols(j), :], w_out_v.at[j], w_out_sem.at[j])

    @pl.loop(0, steps)
    def _(j):
        w_in_copy(j).start()

    def place(index):
        return {"col": 2 * (index // n_depth) + side, "depth": lax.rem(index, n_depth)}

    barrier = pltpu.get_barrier_semaphore()

    @pl.when(row > 0)
    def _():
        pl.semaphore_signal(barrier, inc=1, device_id={"row": row - 1}, device_id_type=MESH)

    @pl.when(row < last_row)
    def _():
        pl.semaphore_signal(barrier, inc=1, device_id={"row": row + 1}, device_id_type=MESH)

    pl.semaphore_signal(barrier, inc=1, device_id={"col": mate}, device_id_type=MESH)
    for k in range(1, group):
        pl.semaphore_signal(
            barrier, inc=1, device_id=place(lax.rem(me + k, group)), device_id_type=MESH
        )
    own_rows = pl.ds(pl.multiple_of(depth * slice_rows, slice_rows), slice_rows)
    tok_all[own_rows, :] = tok_ref[...]
    cot_all[own_rows, :] = cot_ref[...]
    acc_out[...] = jnp.zeros_like(acc_out)
    acc_gin[...] = jnp.zeros_like(acc_gin)

    edges = jnp.where(row > 0, 1, 0) + jnp.where(row < last_row, 1, 0)
    pl.semaphore_wait(barrier, group + edges)

    def depth_copy(a, k):
        src, dst = ((tok_ref, tok_all), (cot_ref, cot_all))[a]
        here = pl.multiple_of(side * half_rows, half_rows)
        there = pl.multiple_of(depth * slice_rows + side * half_rows, half_rows)
        return pltpu.make_async_remote_copy(
            src_ref=src.at[pl.ds(here, half_rows), :],
            dst_ref=dst.at[pl.ds(there, half_rows), :],
            send_sem=depth_sems.at[0, a, k - 1],
            recv_sem=depth_sems.at[1, a, k - 1],
            device_id={"depth": lax.rem(depth + k, n_depth)},
            device_id_type=MESH,
        )

    def swap_copy(a, k):
        dst = (tok_all, cot_all)[a]
        origin = lax.rem(depth + n_depth - k, n_depth)
        rows = pl.ds(pl.multiple_of(origin * slice_rows + side * half_rows, half_rows), half_rows)
        return pltpu.make_async_remote_copy(
            src_ref=dst.at[rows, :],
            dst_ref=dst.at[rows, :],
            send_sem=swap_sems.at[0, a, k - 1],
            recv_sem=swap_sems.at[1, a, k - 1],
            device_id={"col": mate},
            device_id_type=MESH,
        )

    def spread(a):
        for k in range(1, n_depth):
            depth_copy(a, k).start()

    def pass_on(a):
        for k in range(1, n_depth):
            depth_copy(a, k).wait_recv()
            swap_copy(a, k).start()

    def arrived(a):
        for k in range(1, n_depth):
            swap_copy(a, k).wait_recv()

    def right_copy(m):
        return pltpu.make_async_remote_copy(
            src_ref=to_right.at[m],
            dst_ref=from_left.at[m],
            send_sem=left_sems.at[0, m],
            recv_sem=left_sems.at[1, m],
            device_id={"row": lax.rem(row + 1, n_row)},
            device_id_type=MESH,
        )

    def left_copy(m):
        return pltpu.make_async_remote_copy(
            src_ref=to_left.at[m],
            dst_ref=from_right.at[m],
            send_sem=right_sems.at[0, m],
            recv_sem=right_sems.at[1, m],
            device_id={"row": lax.rem(row + n_row - 1, n_row)},
            device_id_type=MESH,
        )

    def pair_copy(a, i):
        return pltpu.make_async_remote_copy(
            src_ref=pair_send.at[a, i],
            dst_ref=pair_recv.at[a, i],
            send_sem=pair_sems.at[0, a, i],
            recv_sem=pair_sems.at[1, a, i],
            device_id={"col": mate},
            device_id_type=MESH,
        )

    def part_copy(a, k):
        return pltpu.make_async_remote_copy(
            src_ref=part_send.at[a, lax.rem(me + k, group)],
            dst_ref=part_recv.at[a, k - 1],
            send_sem=part_sems.at[0, a, k - 1],
            recv_sem=part_sems.at[1, a, k - 1],
            device_id=place(lax.rem(me + k, group)),
            device_id_type=MESH,
        )

    def send_pair(a, acc):
        for i in range(n_col // 2):
            rows = pl.ds(pl.multiple_of((2 * i + 1 - side) * block_rows, block_rows), block_rows)
            pair_send[a, i] = acc[rows, :].astype(jnp.bfloat16)
            pair_copy(a, i).start()

    def send_parts(a, acc):
        for i in range(n_col // 2):
            pair_copy(a, i).wait_recv()
            for p in range(n_depth):
                rows = pl.ds(
                    pl.multiple_of((2 * i + side) * block_rows + p * piece_rows, piece_rows),
                    piece_rows,
                )
                part_send[a, i * n_depth + p] = (
                    acc[rows, :]
                    + pair_recv[a, i, p * piece_rows : (p + 1) * piece_rows, :].astype(jnp.float32)
                ).astype(jnp.bfloat16)
        for k in range(1, group):
            part_copy(a, k).start()

    def finish(a, ref):
        result = part_send[a, me].astype(jnp.float32)
        for k in range(1, group):
            part_copy(a, k).wait_recv()
            result = result + part_recv[a, k - 1].astype(jnp.float32)
        ref[...] = result.astype(ref.dtype)

    outs = ((tok_all, tok_out), (cot_all, cot_out), (act_all, act_out), (hid_all, hid_out))

    def keep(a):
        return pltpu.make_async_copy(outs[a][0], outs[a][1], keep_sem.at[a])

    spread(0)
    pass_on(0)
    spread(1)
    arrived(0)
    keep(0).start()

    far = jnp.maximum(row, last_row - row)
    wait_lag = min(steps, HOP * (n_row // 2))

    @pl.loop(0, msgs + HOP * last_row)
    def _(t):
        @pl.when(t < steps)
        def _():
            w_out_copy(t).start()
            w_in_copy(t).wait()
            own[t] = jnp.dot(
                tok_all[...], w_in_v[t], preferred_element_type=jnp.float32
            ).astype(jnp.bfloat16)

        ready = t - wait_lag

        @pl.when(jnp.logical_and(ready >= 0, ready < steps))
        def _():
            w_out_copy(ready).wait()

        @pl.when(t == min(4, steps - 1))
        def _():
            pass_on(1)

        @pl.when(t == steps)
        def _():
            arrived(1)
            keep(1).start()

        @pl.when(jnp.logical_and(t >= steps, t < msgs))
        def _():
            own[t] = contract_cols(cot_all[...], w_out_v[t - steps]).astype(jnp.bfloat16)

        m1 = t - HOP * row

        @pl.when(jnp.logical_and(m1 >= 0, m1 < msgs))
        def _():
            @pl.when(row == 0)
            def _():
                to_right[m1] = own[m1]

            @pl.when(row > 0)
            def _():
                right_copy(m1).wait_recv()

                @pl.when(row < last_row)
                def _():
                    to_right[m1] = (
                        own[m1].astype(jnp.float32) + from_left[m1].astype(jnp.float32)
                    ).astype(jnp.bfloat16)

            @pl.when(row < last_row)
            def _():
                right_copy(m1).start()

        m2 = t - HOP * (last_row - row)

        @pl.when(jnp.logical_and(m2 >= 0, m2 < msgs))
        def _():
            @pl.when(row == last_row)
            def _():
                to_left[m2] = own[m2]

            @pl.when(row < last_row)
            def _():
                left_copy(m2).wait_recv()

                @pl.when(row > 0)
                def _():
                    to_left[m2] = (
                        own[m2].astype(jnp.float32) + from_right[m2].astype(jnp.float32)
                    ).astype(jnp.bfloat16)

            @pl.when(row > 0)
            def _():
                left_copy(m2).start()

        m = t - HOP * far

        @pl.when(jnp.logical_and(m >= 0, m < msgs))
        def _():
            total[...] = own[m].astype(jnp.float32)

            @pl.when(row > 0)
            def _():
                total[...] += from_left[m].astype(jnp.float32)

            @pl.when(row < last_row)
            def _():
                total[...] += from_right[m].astype(jnp.float32)

        @pl.when(jnp.logical_and(m >= 0, m < steps))
        def _():
            value, slope_value = gelu_parts(total[...])
            slope[m] = slope_value
            block = value.astype(jnp.bfloat16)
            act_all[:, cols(m)] = block
            for n in range(0, d_model, TILE):
                acc_out[:, n : n + TILE] += jnp.dot(
                    block, w_out_v[m, :, n : n + TILE], preferred_element_type=jnp.float32
                )

        mo = m - steps

        @pl.when(jnp.logical_and(mo >= 0, mo < steps))
        def _():
            grad = (total[...] * slope[mo]).astype(jnp.bfloat16)
            hid_all[:, cols(mo)] = grad
            for n in range(0, d_model, TILE):
                acc_gin[:, n : n + TILE] += contract_cols(grad, w_in_v[mo, n : n + TILE, :])

        @pl.when(m == steps)
        def _():
            keep(2).start()
            send_pair(0, acc_out)

        @pl.when(m == steps + min(2, steps - 1))
        def _():
            send_parts(0, acc_out)

    keep(3).start()
    send_pair(1, acc_gin)
    finish(0, out_ref)
    send_parts(1, acc_gin)
    finish(1, gin_ref)

    for a in range(4):
        keep(a).wait()
    for a in range(2):
        for k in range(1, n_depth):
            depth_copy(a, k).wait_send()
            swap_copy(a, k).wait_send()
        for i in range(n_col // 2):
            pair_copy(a, i).wait_send()
        for k in range(1, group):
            part_copy(a, k).wait_send()

    @pl.loop(0, msgs)
    def _(m):
        @pl.when(row < last_row)
        def _():
            right_copy(m).wait_send()

        @pl.when(row > 0)
        def _():
            left_copy(m).wait_send()


def exchange(sizes, tokens, w_in, w_out, cotangent):
    n_row, n_col, n_depth = sizes
    slice_rows, d_model = tokens.shape
    rows = slice_rows * n_depth
    ff = w_in.shape[1]
    steps = ff // CHUNK
    msgs = 2 * steps
    group = (n_col // 2) * n_depth
    block_rows = rows // n_col
    piece_rows = block_rows // n_depth
    bf16, f32 = jnp.bfloat16, jnp.float32
    vmem = pl.BlockSpec(memory_space=pltpu.VMEM)
    hbm = pl.BlockSpec(memory_space=pl.ANY)
    dma = pltpu.SemaphoreType.DMA
    return pl.pallas_call(
        functools.partial(kernel, n_row, n_col, n_depth),
        out_shape=(
            jax.ShapeDtypeStruct((piece_rows, d_model), bf16),
            jax.ShapeDtypeStruct((piece_rows, d_model), bf16),
            jax.ShapeDtypeStruct((rows, d_model), bf16),
            jax.ShapeDtypeStruct((rows, d_model), bf16),
            jax.ShapeDtypeStruct((rows, ff), bf16),
            jax.ShapeDtypeStruct((rows, ff), bf16),
        ),
        in_specs=[vmem, hbm, hbm, vmem],
        out_specs=(vmem, vmem, hbm, hbm, hbm, hbm),
        scratch_shapes=[
            pltpu.VMEM((steps, d_model, CHUNK), bf16),
            pltpu.VMEM((steps, CHUNK, d_model), bf16),
            pltpu.VMEM((rows, d_model), bf16),
            pltpu.VMEM((rows, d_model), bf16),
            pltpu.VMEM((msgs, rows, CHUNK), bf16),
            pltpu.VMEM((msgs, rows, CHUNK), bf16),
            pltpu.VMEM((msgs, rows, CHUNK), bf16),
            pltpu.VMEM((msgs, rows, CHUNK), bf16),
            pltpu.VMEM((msgs, rows, CHUNK), bf16),
            pltpu.VMEM((rows, CHUNK), f32),
            pltpu.VMEM((steps, rows, CHUNK), f32),
            pltpu.VMEM((rows, ff), bf16),
            pltpu.VMEM((rows, ff), bf16),
            pltpu.VMEM((rows, d_model), f32),
            pltpu.VMEM((rows, d_model), f32),
            pltpu.VMEM((2, n_col // 2, block_rows, d_model), bf16),
            pltpu.VMEM((2, n_col // 2, block_rows, d_model), bf16),
            pltpu.VMEM((2, group, piece_rows, d_model), bf16),
            pltpu.VMEM((2, group - 1, piece_rows, d_model), bf16),
            dma((steps,)),
            dma((steps,)),
            dma((4,)),
            dma((2, msgs)),
            dma((2, msgs)),
            dma((2, 2, n_depth - 1)),
            dma((2, 2, n_depth - 1)),
            dma((2, 2, n_col // 2)),
            dma((2, 2, group - 1)),
        ],
        compiler_params=pltpu.CompilerParams(
            collective_id=0, has_side_effects=True, vmem_limit_bytes=62 * 2**20
        ),
        cost_estimate=pl.CostEstimate(
            flops=8 * rows * d_model * ff, bytes_accessed=4 * d_model * ff, transcendentals=rows * ff
        ),
        name="exchange",
    )(tokens, w_in, w_out, cotangent)


def grads_kernel(scale, tok, hid, act, cot, out, gin, g_in, g_out, out_copy, gin_copy):
    @pl.when(pl.program_id(0) == 0)
    def _():
        out_copy[...] = out[...]
        gin_copy[...] = gin[...]

    for left, right, result in ((tok, hid, g_in), (act, cot, g_out)):
        turned = left[...].T
        for n in range(0, right.shape[1], TILE):
            result[:, n : n + TILE] = (
                jnp.dot(turned, right[:, n : n + TILE], preferred_element_type=jnp.float32) * scale
            ).astype(result.dtype)


def weight_grads(tokens, hidden, act, grads, output, grad_input):
    rows, d_model = tokens.shape
    ff = hidden.shape[1]
    bf16 = jnp.bfloat16
    count = max(d_model, ff) // GRAD_ROWS
    small = pl.BlockSpec(output.shape, lambda i: (0, 0))
    return pl.pallas_call(
        functools.partial(grads_kernel, rows ** (-0.5)),
        grid=(count,),
        out_shape=(
            jax.ShapeDtypeStruct((d_model, ff), bf16),
            jax.ShapeDtypeStruct((ff, d_model), bf16),
            jax.ShapeDtypeStruct(output.shape, bf16),
            jax.ShapeDtypeStruct(grad_input.shape, bf16),
        ),
        in_specs=[
            pl.BlockSpec((rows, d_model // count), lambda i: (0, i)),
            pl.BlockSpec((rows, ff), lambda i: (0, 0)),
            pl.BlockSpec((rows, ff // count), lambda i: (0, i)),
            pl.BlockSpec((rows, d_model), lambda i: (0, 0)),
            small,
            small,
        ],
        out_specs=(
            pl.BlockSpec((d_model // count, ff), lambda i: (i, 0)),
            pl.BlockSpec((ff // count, d_model), lambda i: (i, 0)),
            small,
            small,
        ),
        compiler_params=pltpu.CompilerParams(vmem_limit_bytes=62 * 2**20),
        cost_estimate=pl.CostEstimate(
            flops=4 * rows * d_model * ff, bytes_accessed=4 * d_model * ff, transcendentals=0
        ),
        name="weight_grads",
    )(tokens, hidden, act, grads, output, grad_input)


def body(sizes, tokens, w_in, w_out, cotangent):
    output, grad_input, all_tokens, all_grads, act, hidden = exchange(
        sizes, tokens, w_in, w_out, cotangent
    )
    grad_w_in, grad_w_out, output, grad_input = weight_grads(
        all_tokens, hidden, act, all_grads, output, grad_input
    )
    return (output, grad_input, grad_w_in, grad_w_out)


def solution(mesh):
    sizes = (mesh.shape["row"], mesh.shape["col"], mesh.shape["depth"])
    in_specs = (
        P("depth", "row"),
        P("row", ("col", "depth")),
        P(("col", "depth"), "row"),
        P("depth", "row"),
    )
    out_specs = (
        P(("col", "depth"), "row"),
        P(("col", "depth"), "row"),
        P("row", ("col", "depth")),
        P(("col", "depth"), "row"),
    )
    return jax.shard_map(
        functools.partial(body, sizes),
        mesh=mesh,
        in_specs=in_specs,
        out_specs=out_specs,
        check_vma=False,
    )
```
